32 devices in a mesh: sec: 4 (over z), dev: 8 (over y, x, core).
Axes of the slice: x: 2, y: 2, z: 4, core: 2. Of those that a mesh axis runs over, the one named last changes fastest.
Arguments:
- x_input: bfloat16 [65536, 2048], P(('sec', 'dev'))
- log_decay: float32 [65536, 32], P(('sec', 'dev')), as said below
- b_input: bfloat16 [65536, 64], P(('sec', 'dev')), may hold values from -6 to 6
- c_input: bfloat16 [65536, 64], P(('sec', 'dev')), may hold values from -0.75 to 0.75
- skip_gain: float32 [32], replicated, may hold values from 0.5 to 2
- score_weight: bfloat16 [2048], replicated, may hold values from -0.125 to 0.125
- trace_lengths: int32 [4], replicated, may hold values from 1 to 32768, 65536 in all
- step_lengths: int32 [512], replicated, may hold values from 1 to 512, 65536 in all
- step_slot: int32 [512], replicated, may hold values from 0 to 511, each once
Outputs:
- y_output: bfloat16 [65536, 2048], P(('sec', 'dev'))
- step_scores: float32 [512], P(('sec', 'dev'))
The draws below stay inside these ranges and needn't reach their ends.
Inputs may be any that keep to these rules, and one draw needn't show every extreme that they name: `trace_lengths`: the lengths sum to 65536; one trace has exactly 32768 tokens. `step_lengths`: the lengths sum to 65536; some step has exactly 512 tokens. `step_slot`: each slot is named by exactly one step. `log_decay`: every entry is negative.
All inputs are finite; a program needn't handle non-finite values.
Results may differ from the reference program's by a relative error of at most 0.0053.
Values sent between devices are 32-bit elements; how exact they have to be, the bound alone decides.
A program may use at most 384 MiB of HBM per device.

```python
import math
import jax
import jax.numpy as jnp
import numpy as np
from jax import lax

H = 32
P_SIZE = 64
N = 64
GROUP = 256
TRACES = 4
STEP_MOST = 512
TOK_DEV = 2048
TOKENS = 65536
STEPS = 512


def head_rates(key):
    kind = jax.random.uniform(jax.random.fold_in(key, 11), (H,))
    share = 0.5
    top = 6.0
    slow = kind < share
    slow_rate = jnp.exp(jax.random.uniform(jax.random.fold_in(key, 12), (H,), minval=math.log(0.25), maxval=math.log(top))) / TOKENS
    fast_rate = 1.0 / jnp.exp(jax.random.uniform(jax.random.fold_in(key, 13), (H,), minval=math.log(30.0), maxval=math.log(50.0)))
    return jnp.where(slow, slow_rate, fast_rate)


def draw_log_decay(key, part):
    attenuation_speeds = head_rates(key)
    position_attenuation_multiplier = jnp.exp(jax.random.uniform(jax.random.fold_in(key, 21), (TOKENS, H), minval=math.log(0.5), maxval=math.log(2.0)))
    blocks = TOKENS // TOK_DEV
    tile_attenuation_multiplier = jnp.exp(jax.random.uniform(jax.random.fold_in(key, 22), (blocks, H), minval=math.log(0.5), maxval=math.log(2.0)))
    tile_attenuation_multiplier = jnp.repeat(tile_attenuation_multiplier, TOK_DEV, axis=0)
    places = jax.random.randint(jax.random.fold_in(key, 23), (4,), 0, TOKENS)
    piece_extents = jnp.exp(jax.random.uniform(jax.random.fold_in(key, 24), (4,), minval=math.log(0.22), maxval=math.log(0.7)))
    equality_indicator = jnp.arange(TOKENS, dtype=jnp.int32)[:, None] == places[None, :]
    contiguous_span_piece = jnp.sum(jnp.where(equality_indicator, piece_extents[None, :], 0.0), axis=1)
    payload_vectors = -(attenuation_speeds[None, :] * position_attenuation_multiplier * tile_attenuation_multiplier) - contiguous_span_piece[:, None]
    return payload_vectors.astype(jnp.float32)


def draw_x_input(key, part):
    attenuation_speeds = head_rates(key)
    sigma = jnp.sqrt(2.0 * jnp.maximum(attenuation_speeds, 2.0 / TOKENS))
    noise = jax.random.normal(jax.random.fold_in(key, 31), (TOKENS, H, P_SIZE))
    payload_vectors = noise * sigma[None, :, None]
    return payload_vectors.reshape(TOKENS, H * P_SIZE).astype(jnp.bfloat16)


def block_scale(key, extent, split, least, largest):
    loudness, own = 1.0, jax.random.fold_in(key, 6)
    for dim, shards_of in split:
        steps = jnp.exp(jax.random.uniform(jax.random.fold_in(own, dim), (shards_of,), jnp.float32, least / len(split), largest / len(split)))
        loudness = loudness * jnp.repeat(steps, extent[dim] // shards_of).reshape([-1 if axis == dim else 1 for axis in range(len(extent))])
    return loudness


def split_up(count, total, limit, skew):
    weights = [(1 << 20) // math.isqrt(standing ** skew) + 1 for standing in range(2, count + 1)]
    spare, holding = total - limit - (count - 1), [1] * (count - 1)
    while spare > 0:
        movable = [i for i in range(count - 1) if holding[i] < limit]
        whole, budget = sum([weights[i] for i in movable]), spare
        for i in movable:
            extra = min(limit - holding[i], max(1, budget * weights[i] // whole), spare)
            holding[i] = holding[i] + extra
            spare = spare - extra
    return np.array([limit] + holding)


def ragged_sizes(key, count, total, bound, slope):
    if count == 2:
        one = jax.random.randint(key, (), max(1, total - bound), min(bound, total - 1) + 1)
        return jnp.stack([one, total - one])
    sizes = jnp.asarray(split_up(count, total, bound, slope), jnp.int32)
    pairs = (count - 1) // 2
    donor, sink = sizes[1:1 + 2 * pairs:2], sizes[2:2 + 2 * pairs:2]
    room = jnp.minimum(donor - 1, bound - sink)
    moved = jax.random.randint(jax.random.fold_in(key, 1), (pairs,), 0, 1 << 20) % (room + 1)
    sizes = sizes.at[1:1 + 2 * pairs:2].set(donor - moved).at[2:2 + 2 * pairs:2].set(sink + moved)
    return sizes[jax.random.permutation(jax.random.fold_in(key, 2), count)]


def bell_draw(own_key, shape, deviation, most, split=(), kind=jnp.bfloat16):
    result = deviation * jax.random.normal(own_key, shape, jnp.float32)
    if split:
        result = result * block_scale(own_key, shape, split, -0.22, 0.18)
    return jnp.clip(result, -most, most).astype(kind)


def setup_inputs(seed: int = 0) -> dict:
    seeds = jax.random.split(jax.random.key(seed), 10)
    x_input = draw_x_input(jax.random.fold_in(seeds[9], 71), 0)
    log_decay = draw_log_decay(jax.random.fold_in(seeds[9], 71), 0)
    b_input = bell_draw(seeds[2], (TOKENS, N), 1.0, 6.0, ((0, 32),))
    c_input = bell_draw(seeds[3], (TOKENS, N), N ** -0.5, 0.75, ((0, 32),))
    skip_gain = jnp.clip(jax.random.uniform(seeds[4], (H,), jnp.float32, 0.5, 2.0), 0.5, 2.0)
    score_weight = bell_draw(seeds[5], (H * P_SIZE,), (H * P_SIZE) ** -0.5, 0.125)
    trace_lengths = ragged_sizes(seeds[6], TRACES, TOKENS, TOKENS // 2, 1).astype(jnp.int32)
    step_lengths = ragged_sizes(seeds[7], STEPS, TOKENS, STEP_MOST, 2).astype(jnp.int32)
    step_slot = jax.random.permutation(seeds[8], STEPS).astype(jnp.int32)
    return {"x_input": x_input, "log_decay": log_decay, "b_input": b_input, "c_input": c_input, "skip_gain": skip_gain, "score_weight": score_weight, "trace_lengths": trace_lengths, "step_lengths": step_lengths, "step_slot": step_slot}


def trace_ids(starts, positions):
    return jnp.sum((starts[None, :] <= positions[:, None]).astype(jnp.int32), axis=1)


def group_terms(x_group, decay_group, b_group, c_group, trace_group, prev_trace):
    length = x_group.shape[0]
    cum = jnp.cumsum(decay_group, axis=0)
    cum_heads = cum.T
    order = jnp.arange(length, dtype=jnp.int32)
    keep = (order[:, None] >= order[None, :]) & (trace_group[:, None] == trace_group[None, :])
    gram = jnp.dot(c_group, b_group.T, preferred_element_type=jnp.float32)
    diff = cum_heads[:, :, None] - cum_heads[:, None, :]
    decay = jnp.exp(jnp.where(keep[None], diff, -jnp.inf))
    weight = lax.optimization_barrier((gram[None] * decay).astype(jnp.bfloat16))
    x_heads = x_group.reshape(length, H, P_SIZE)
    intra = jnp.einsum("hts,shp->thp", weight.astype(jnp.float32), x_heads.astype(jnp.float32))
    to_end = jnp.exp(cum[-1][None, :] - cum) * (trace_group == trace_group[-1]).astype(jnp.float32)[:, None]
    scaled = lax.optimization_barrier((x_heads.astype(jnp.float32) * to_end[:, :, None]).astype(jnp.bfloat16))
    new_state = jnp.einsum("shp,sn->hpn", scaled.astype(jnp.float32), b_group.astype(jnp.float32))
    carry = jnp.exp(cum) * (trace_group == prev_trace).astype(jnp.float32)[:, None]
    return intra, new_state, carry


def reference(x_input, log_decay, b_input, c_input, skip_gain, score_weight, trace_lengths, step_lengths, step_slot):
    count = TOKENS // GROUP
    positions = jnp.arange(TOKENS, dtype=jnp.int32)
    starts = (jnp.cumsum(trace_lengths) - trace_lengths).astype(jnp.int32)
    trace = trace_ids(starts, positions).reshape(count, GROUP)
    prev = trace_ids(starts, (jnp.arange(count, dtype=jnp.int32) * GROUP - 1).astype(jnp.int32))
    inputs = (x_input.reshape(count, GROUP, H * P_SIZE), log_decay.reshape(count, GROUP, H),
              b_input.reshape(count, GROUP, N), c_input.reshape(count, GROUP, N), trace, prev)

    def advance(state, item):
        x_group, decay_group, b_group, c_group, trace_group, prev_trace = item
        intra, new_state, carry = group_terms(x_group, decay_group, b_group, c_group, trace_group, prev_trace)
        read_state = lax.optimization_barrier(state.astype(jnp.bfloat16))
        inter = jnp.einsum("tn,hpn->thp", c_group.astype(jnp.float32), read_state.astype(jnp.float32)) * carry[:, :, None]
        x_heads = x_group.reshape(GROUP, H, P_SIZE).astype(jnp.float32)
        y_group = (intra + inter + skip_gain[None, :, None] * x_heads).astype(jnp.bfloat16).reshape(GROUP, H * P_SIZE)
        following = carry[-1][:, None, None] * state + new_state
        return following, y_group

    first = jnp.zeros((H, P_SIZE, N), jnp.float32)
    last, y_blocks = lax.scan(advance, first, inputs)
    y_output = y_blocks.reshape(TOKENS, H * P_SIZE)
    score = jnp.dot(y_output, score_weight, preferred_element_type=jnp.float32)
    step_starts = (jnp.cumsum(step_lengths) - step_lengths).astype(jnp.int32)
    step_id = (jnp.searchsorted(step_starts, positions, side="right") - 1).astype(jnp.int32)
    totals = jax.ops.segment_sum(score, step_id, num_segments=STEPS)
    pooled = totals / step_lengths.astype(jnp.float32)
    step_scores = jnp.zeros((STEPS,), jnp.float32).at[step_slot].set(pooled)
    return y_output, step_scores
```

```python
import functools
import math

import jax
import jax.numpy as jnp
from jax import lax
from jax.experimental import pallas as pl
from jax.experimental.pallas import tpu as pltpu
from jax.sharding import PartitionSpec as P

CHUNK = 128
LANES = 128
LOG2E = 1.0 / math.log(2.0)
F32 = jnp.float32
BF16 = jnp.bfloat16
VMEM_BYTES = 48 * 1024 * 1024


def iota(shape, dim):
    return lax.broadcasted_iota(jnp.int32, shape, dim)


def my_index():
    return lax.axis_index("sec") * lax.axis_size("dev") + lax.axis_index("dev")


def trace_at(lengths_ref, positions):
    start = jnp.int32(0)
    found = jnp.zeros(jnp.shape(positions), jnp.int32)
    for i in range(lengths_ref.shape[0]):
        found = found + jnp.where(positions >= start, 1, 0)
        start = start + lengths_ref[i]
    return found


def running(decay):
    ones = jnp.where(iota((CHUNK, CHUNK), 0) >= iota((CHUNK, CHUNK), 1), 1.0, 0.0).astype(F32)
    cum = jnp.dot(ones, decay, precision=lax.Precision.HIGHEST, preferred_element_type=F32)
    return cum * LOG2E


def halves(value):
    high = value.astype(BF16)
    low = (value - high.astype(F32)).astype(BF16)
    return jnp.concatenate([high, low], axis=1)


def spread_matrix(heads, width):
    size = width // heads
    row = iota((2 * heads, width), 0)
    head = jnp.where(row >= heads, row - heads, row)
    column = iota((2 * heads, width), 1)
    inside = (column >= head * size) & (column < (head + 1) * size)
    return jnp.where(inside, 1.0, 0.0).astype(BF16)


def state_kernel(count, groups, lengths, x_ref, decay_ref, b_ref, enter_ref, before_ref, send_ref,
                 spread, state, factor):
    k = pl.program_id(0)
    heads, width = decay_ref.shape[1], x_ref.shape[1]

    @pl.when(k == 0)
    def _():
        spread[...] = spread_matrix(heads, width)
        state[...] = jnp.zeros_like(state)
        factor[...] = jnp.ones_like(factor)

    first = (my_index() * count + k) * CHUNK
    cum = running(decay_ref[...])
    trace = trace_at(lengths, first + iota((CHUNK, 1), 0))
    last_trace = trace_at(lengths, jnp.full((1, 1), first + CHUNK - 1, jnp.int32))
    prev_trace = trace_at(lengths, jnp.full((1, 1), first - 1, jnp.int32))
    end = cum[CHUNK - 1:, :]
    to_end = jnp.exp2(end - cum) * jnp.where(trace == last_trace, 1.0, 0.0)
    through = jnp.exp2(end) * jnp.where(last_trace == prev_trace, 1.0, 0.0)
    small = jnp.concatenate([to_end, jnp.broadcast_to(through, (16, heads))], axis=0)
    wide = jnp.dot(halves(small), spread[...], preferred_element_type=F32)
    scaled = (x_ref[...].astype(F32) * wide[:CHUNK]).astype(BF16)
    new = lax.dot_general(b_ref[...], scaled, (((0,), (0,)), ((), ())), preferred_element_type=F32)
    pass_on = wide[CHUNK:CHUNK + 8]
    enter_ref[0] = state[...].astype(BF16)
    before_ref[0] = factor[...]
    state[...] = state[...] * pass_on[:1] + new
    factor[...] = factor[...] * pass_on

    @pl.when(k == count - 1)
    def _():
        rows = state.shape[0] // groups
        for pair in range(width // LANES):
            columns = slice(pair * LANES, (pair + 1) * LANES)
            for g in range(groups):
                send_ref[pair * groups + g, :rows, :] = state[g * rows:(g + 1) * rows, columns]
                send_ref[pair * groups + g, rows:, :] = factor[:, columns]


def greet_all(devices, coords):
    me = my_index()
    barrier = pltpu.get_barrier_semaphore()

    def greet(off, _):
        pl.semaphore_signal(barrier, inc=1, device_id=coords(lax.rem(me + off, devices)),
                            device_id_type=pl.DeviceIdType.MESH)
        return 0

    lax.fori_loop(1, devices, greet, 0)
    pl.semaphore_wait(barrier, devices - 1)


def coordinates(device):
    across = lax.axis_size("dev")
    return (lax.div(device, across), lax.rem(device, across))


def exchange_kernel(devices, groups, send_ref, out_ref, arrived, answers, returned,
                    send_a, recv_a, send_b, recv_b):
    me = my_index()
    rows = answers.shape[1]
    greet_all(devices, coordinates)

    def there(off):
        device = lax.rem(me + off, devices)
        return pltpu.make_async_remote_copy(
            src_ref=send_ref.at[device], dst_ref=arrived.at[me],
            send_sem=send_a.at[off], recv_sem=recv_a.at[off],
            device_id=coordinates(device), device_id_type=pl.DeviceIdType.MESH)

    def back(off):
        device = lax.rem(me + off, devices)
        return pltpu.make_async_remote_copy(
            src_ref=answers.at[device], dst_ref=returned.at[me],
            send_sem=send_b.at[off], recv_sem=recv_b.at[off],
            device_id=coordinates(device), device_id_type=pl.DeviceIdType.MESH)

    def begin(copy):
        def one(off, _):
            copy(off).start()
            return 0
        lax.fori_loop(1, devices, one, 0)

    def finish(copy):
        def one(off, _):
            copy(off).wait()
            return 0
        lax.fori_loop(1, devices, one, 0)

    begin(there)
    arrived[me] = send_ref[me]
    finish(there)

    def step(i, held):
        answers[i] = held
        part = arrived[i]
        return held * part[rows:rows + 1] + part[:rows]

    lax.fori_loop(0, devices, step, jnp.zeros(answers.shape[1:], F32))
    begin(back)
    returned[me] = answers[me]
    finish(back)
    for pair in range(devices // groups):
        for g in range(groups):
            out_ref[g * rows:(g + 1) * rows, pair * LANES:(pair + 1) * LANES] = returned[
                pair * groups + g]


def output_kernel(count, lengths, x_ref, decay_ref, b_ref, c_ref, incoming_ref, enter_ref,
                  before_ref, gain_ref, score_ref, steps_ref, y_ref, part_ref,
                  spread, gain, starts):
    k = pl.program_id(0)
    heads, width = decay_ref.shape[1], x_ref.shape[1]
    lines = steps_ref.shape[0]

    @pl.when(k == 0)
    def _():
        spread[...] = spread_matrix(heads, width)
        gain[...] = jnp.dot(halves(jnp.broadcast_to(gain_ref[...], (16, heads))), spread[...],
                            preferred_element_type=F32)[:8]
        sizes = steps_ref[...].astype(F32)
        upper = jnp.where(iota((LANES, LANES), 0) < iota((LANES, LANES), 1), 1.0, 0.0).astype(F32)
        inner = jnp.dot(sizes, upper, precision=lax.Precision.HIGHEST, preferred_element_type=F32)
        total = jnp.sum(sizes, axis=1, keepdims=True)
        offset = jnp.zeros((1, 1), F32)
        for i in range(lines):
            starts[i:i + 1, :] = inner[i:i + 1, :] + offset
            offset = offset + total[i:i + 1, :]
        part_ref[...] = jnp.zeros_like(part_ref)

    first = (my_index() * count + k) * CHUNK
    cum = running(decay_ref[...])
    cum_rows = cum.T
    trace = trace_at(lengths, first + iota((CHUNK, 1), 0))
    trace_row = trace_at(lengths, first + iota((1, CHUNK), 1))
    prev_trace = trace_at(lengths, jnp.full((1, 1), first - 1, jnp.int32))
    keep = (iota((CHUNK, CHUNK), 0) >= iota((CHUNK, CHUNK), 1)) & (trace == trace_row)
    gram = lax.dot_general(c_ref[...], b_ref[...], (((1,), (1,)), ((), ())),
                           preferred_element_type=F32)
    gram = jnp.where(keep, gram, 0.0)
    carry = halves(jnp.exp2(cum) * jnp.where(trace == prev_trace, 1.0, 0.0))
    low_half = iota((CHUNK, LANES), 1) < LANES // 2
    quad = 2 * LANES
    scores = jnp.zeros((CHUNK, quad), F32)
    per_pair = LANES * heads // width

    def weight(h):
        diff = jnp.minimum(cum[:, h:h + 1] - cum_rows[h:h + 1, :], 0.0)
        return (gram * jnp.exp2(diff)).astype(BF16)

    for q in range(width // quad):
        columns = slice(q * quad, (q + 1) * quad)
        full = (before_ref[0, :1, columns] * incoming_ref[:, columns]
                + enter_ref[0, :, columns].astype(F32)).astype(BF16)
        inter = jnp.dot(c_ref[...], full, preferred_element_type=F32)
        wide = jnp.dot(carry, spread[:, columns], preferred_element_type=F32)
        pieces = []
        for pair in range(2 * q, 2 * q + 2):
            x_pair = x_ref[:, pair * LANES:(pair + 1) * LANES]
            zero = jnp.zeros_like(x_pair)
            both = jnp.concatenate(
                [jnp.where(low_half, x_pair, zero), jnp.where(low_half, zero, x_pair)], axis=0)
            weights = jnp.concatenate([weight(per_pair * pair), weight(per_pair * pair + 1)], axis=1)
            pieces.append(jnp.dot(weights, both, preferred_element_type=F32))
        intra = jnp.concatenate(pieces, axis=1)
        y = (intra + wide * inter + gain[:1, columns] * x_ref[:, columns].astype(F32)).astype(BF16)
        y_ref[:, columns] = y
        scores = scores + y.astype(F32) * score_ref[:1, columns].astype(F32)

    score = jnp.sum(scores, axis=1, keepdims=True)
    places = (first + iota((CHUNK, 1), 0)).astype(F32)
    sizes = steps_ref[...].astype(F32)
    for i in range(lines):
        start = starts[i:i + 1, :]
        inside = (start <= places) & (places < start + sizes[i:i + 1, :])
        part_ref[i:i + 1, :] += jnp.sum(jnp.where(inside, score, 0.0), axis=0, keepdims=True)


def pool_kernel(devices, owned, part_ref, steps_ref, slot_ref, out_ref, arrived, send, recv):
    me = my_index()
    lines = steps_ref.shape[0]
    greet_all(devices, coordinates)

    def copy(off):
        device = lax.rem(me + off, devices)
        return pltpu.make_async_remote_copy(
            src_ref=part_ref, dst_ref=arrived.at[me],
            send_sem=send.at[off], recv_sem=recv.at[off],
            device_id=coordinates(device), device_id_type=pl.DeviceIdType.MESH)

    def begin(off, _):
        copy(off).start()
        return 0

    def finish(off, _):
        copy(off).wait()
        return 0

    lax.fori_loop(1, devices, begin, 0)
    arrived[me] = part_ref[...]
    lax.fori_loop(1, devices, finish, 0)
    total = lax.fori_loop(0, devices, lambda i, t: t + arrived[i], jnp.zeros(part_ref.shape, F32))
    mean = total[:lines] / steps_ref[...].astype(F32)
    slots = me * owned + iota((owned, LANES), 0)
    found = jnp.zeros((owned, LANES), F32)
    for i in range(lines):
        found = found + jnp.where(slot_ref[i:i + 1, :] == slots, mean[i:i + 1, :], 0.0)
    out_ref[...] = jnp.broadcast_to(jnp.sum(found, axis=1, keepdims=True), (owned, LANES))


def shards(x_input, log_decay, b_input, c_input, skip_gain, score_weight, trace_lengths,
           step_lengths, step_slot):
    rows, width = x_input.shape
    heads = log_decay.shape[1]
    state_size = b_input.shape[1]
    count = rows // CHUNK
    devices = lax.axis_size(("sec", "dev"))
    groups = devices // (width // LANES)
    depth = state_size // groups
    steps = step_slot.shape[0]
    lines = steps // LANES
    owned = steps // devices
    whole = pl.BlockSpec(memory_space=pltpu.VMEM)
    scalar = pl.BlockSpec(memory_space=pltpu.SMEM)

    def by_chunk(columns):
        return pl.BlockSpec((CHUNK, columns), lambda k: (k, 0))

    def by_chunk3(a, b):
        return pl.BlockSpec((1, a, b), lambda k: (k, 0, 0))

    def fixed(*shape):
        return pl.BlockSpec(shape, lambda k: (0,) * len(shape))

    enter, before, send = pl.pallas_call(
        functools.partial(state_kernel, count, groups),
        grid=(count,),
        in_specs=[scalar, by_chunk(width), by_chunk(heads), by_chunk(state_size)],
        out_specs=[by_chunk3(state_size, width), by_chunk3(8, width),
                   fixed(devices, depth + 8, LANES)],
        out_shape=[jax.ShapeDtypeStruct((count, state_size, width), BF16),
                   jax.ShapeDtypeStruct((count, 8, width), F32),
                   jax.ShapeDtypeStruct((devices, depth + 8, LANES), F32)],
        scratch_shapes=[pltpu.VMEM((2 * heads, width), BF16), pltpu.VMEM((state_size, width), F32),
                        pltpu.VMEM((8, width), F32)],
        compiler_params=pltpu.CompilerParams(vmem_limit_bytes=VMEM_BYTES),
        name="chunk_states",
    )(trace_lengths, x_input, log_decay, b_input)

    sems = pltpu.SemaphoreType.DMA((devices,))
    incoming = pl.pallas_call(
        functools.partial(exchange_kernel, devices, groups),
        in_specs=[whole],
        out_specs=whole,
        out_shape=jax.ShapeDtypeStruct((state_size, width), F32),
        scratch_shapes=[pltpu.VMEM((devices, depth + 8, LANES), F32),
                        pltpu.VMEM((devices, depth, LANES), F32),
                        pltpu.VMEM((devices, depth, LANES), F32), sems, sems, sems, sems],
        compiler_params=pltpu.CompilerParams(collective_id=0, has_side_effects=True,
                                             vmem_limit_bytes=VMEM_BYTES),
        name="state_exchange",
    )(send)

    lines8 = max(8, lines)
    steps_rows = step_lengths.reshape(lines, LANES)
    y_output, part = pl.pallas_call(
        functools.partial(output_kernel, count),
        grid=(count,),
        in_specs=[scalar, by_chunk(width), by_chunk(heads), by_chunk(state_size),
                  by_chunk(state_size), fixed(state_size, width), by_chunk3(state_size, width),
                  by_chunk3(8, width), fixed(1, heads), fixed(1, width), fixed(lines, LANES)],
        out_specs=[by_chunk(width), fixed(lines8, LANES)],
        out_shape=[jax.ShapeDtypeStruct((rows, width), BF16),
                   jax.ShapeDtypeStruct((lines8, LANES), F32)],
        scratch_shapes=[pltpu.VMEM((2 * heads, width), BF16), pltpu.VMEM((8, width), F32),
                        pltpu.VMEM((lines8, LANES), F32)],
        compiler_params=pltpu.CompilerParams(vmem_limit_bytes=VMEM_BYTES),
        name="outputs",
    )(trace_lengths, x_input, log_decay, b_input, c_input, incoming, enter, before,
      skip_gain.reshape(1, heads), score_weight.reshape(1, width), steps_rows)

    pooled = pl.pallas_call(
        functools.partial(pool_kernel, devices, owned),
        in_specs=[whole, whole, whole],
        out_specs=whole,
        out_shape=jax.ShapeDtypeStruct((owned, LANES), F32),
        scratch_shapes=[pltpu.VMEM((devices, lines8, LANES), F32), sems, sems],
        compiler_params=pltpu.CompilerParams(collective_id=1, has_side_effects=True,
                                             vmem_limit_bytes=VMEM_BYTES),
        name="step_pool",
    )(part, steps_rows, step_slot.reshape(lines, LANES))
    return (y_output, pooled[:, 0])


def solution(mesh):
    tokens = P(("sec", "dev"), None)
    return jax.shard_map(
        shards,
        mesh=mesh,
        in_specs=(tokens, tokens, tokens, tokens, P(), P(), P(), P(), P()),
        out_specs=(tokens, P(("sec", "dev"))),
        check_vma=False,
    )
```

```python
import functools
import math

import jax
import jax.numpy as jnp
from jax import lax
from jax.experimental import pallas as pl
from jax.experimental.pallas import tpu as pltpu
from jax.sharding import PartitionSpec as P

CHUNK = 128
STATE_CHUNKS = 4
OUTPUT_CHUNKS = 2
LANES = 128
LOG2E = 1.0 / math.log(2.0)
F32 = jnp.float32
BF16 = jnp.bfloat16
VMEM_BYTES = 60 * 1024 * 1024


def iota(shape, dim):
    return lax.broadcasted_iota(jnp.int32, shape, dim)


def my_index():
    return lax.axis_index("sec") * lax.axis_size("dev") + lax.axis_index("dev")


def trace_at(lengths_ref, positions):
    start = jnp.int32(0)
    found = jnp.zeros(jnp.shape(positions), jnp.int32)
    for i in range(lengths_ref.shape[0]):
        found = found + jnp.where(positions >= start, 1, 0)
        start = start + lengths_ref[i]
    return found


def running(decay_rows):
    ones = jnp.where(iota((CHUNK, CHUNK), 0) <= iota((CHUNK, CHUNK), 1), 1.0, 0.0).astype(F32)
    cum = jnp.dot(decay_rows, ones, precision=lax.Precision.HIGHEST, preferred_element_type=F32)
    return cum * LOG2E


def halves(value):
    high = value.astype(BF16)
    low = (value - high.astype(F32)).astype(BF16)
    return jnp.concatenate([high, low], axis=1)


def spread_matrix(heads, width):
    size = width // heads
    row = iota((2 * heads, width), 0)
    head = jnp.where(row >= heads, row - heads, row)
    column = iota((2 * heads, width), 1)
    inside = (column >= head * size) & (column < (head + 1) * size)
    return jnp.where(inside, 1.0, 0.0).astype(BF16)


def state_kernel(count, groups, lengths, x_ref, decay_ref, b_ref, enter_ref, before_ref, send_ref,
                 spread, state, factor):
    k = pl.program_id(0)
    heads, width = decay_ref.shape[0], x_ref.shape[1]

    @pl.when(k == 0)
    def _():
        spread[...] = spread_matrix(heads, width)
        state[...] = jnp.zeros_like(state)
        factor[...] = jnp.ones_like(factor)

    ends, passes = [], jnp.zeros((heads, LANES), F32)
    for sub in range(STATE_CHUNKS):
        tokens = slice(sub * CHUNK, (sub + 1) * CHUNK)
        first = (my_index() * count + k * STATE_CHUNKS + sub) * CHUNK
        cum = running(decay_ref[:, tokens])
        trace = trace_at(lengths, first + iota((1, CHUNK), 1))
        last_trace = trace_at(lengths, jnp.full((1, 1), first + CHUNK - 1, jnp.int32))
        prev_trace = trace_at(lengths, jnp.full((1, 1), first - 1, jnp.int32))
        end = cum[:, CHUNK - 1:]
        ends.append(jnp.exp2(end - cum) * jnp.where(trace == last_trace, 1.0, 0.0))
        through = jnp.exp2(end) * jnp.where(last_trace == prev_trace, 1.0, 0.0)
        passes = passes + jnp.where(iota((heads, LANES), 1) == sub, through, 0.0)
    pass_on = jnp.dot(halves(passes.T[:16]), spread[...], preferred_element_type=F32)

    inputs = [b_ref[:, sub * CHUNK:(sub + 1) * CHUNK].astype(F32) for sub in range(STATE_CHUNKS)]
    states = state.shape[0]
    low_half = iota((states, LANES), 1) < LANES // 2
    for pair in range(width // LANES):
        columns = slice(pair * LANES, (pair + 1) * LANES)
        held, product = state[:, columns], factor[:, columns]
        for sub in range(STATE_CHUNKS):
            tokens = slice(sub * CHUNK, (sub + 1) * CHUNK)
            both = jnp.concatenate(
                [(inputs[sub] * ends[sub][h:h + 1, :]).astype(BF16) for h in (2 * pair, 2 * pair + 1)],
                axis=0)
            new = jnp.dot(both, x_ref[tokens, columns], preferred_element_type=F32)
            step = pass_on[sub:sub + 1, columns]
            enter_ref[sub, :, columns] = held.astype(BF16)
            before_ref[sub, :, columns] = product
            held = held * step + jnp.where(low_half, new[:states], new[states:])
            product = product * step
        state[:, columns] = held
        factor[:, columns] = product

    @pl.when(k == count // STATE_CHUNKS - 1)
    def _():
        rows = state.shape[0] // groups
        for pair in range(width // LANES):
            columns = slice(pair * LANES, (pair + 1) * LANES)
            for g in range(groups):
                send_ref[pair * groups + g, :rows, :] = state[g * rows:(g + 1) * rows, columns]
                send_ref[pair * groups + g, rows:, :] = factor[:, columns]


def wrapped(index, size):
    return index - jnp.where(index >= size, size, 0)


def each(low, high, action):
    def one(i, _):
        action(i)
        return 0

    lax.fori_loop(low, high, one, 0)


def greet(coords):
    pl.semaphore_signal(pltpu.get_barrier_semaphore(), inc=1, device_id=coords,
                        device_id_type=pl.DeviceIdType.MESH)


def exchange_kernel(chips, groups, send_ref, out_ref, other, chip, arrived, answers, returned,
                    theirs, last, pair_send, pair_recv, send_a, recv_a, send_b, recv_b):
    sec, dev = lax.axis_index("sec"), lax.axis_index("dev")
    per_sec = lax.axis_size("dev") // 2
    core = lax.rem(dev, 2)
    here = sec * per_sec + lax.div(dev, 2)
    early = core == 0
    partner = (sec, dev + 1 - 2 * core)
    rows = answers.shape[1]

    def peer(off):
        place = wrapped(here + off, chips)
        return place, (lax.div(place, per_sec), lax.rem(place, per_sec) * 2 + core)

    each(1, chips, lambda off: greet(peer(off)[1]))
    greet(partner)
    pl.semaphore_wait(pltpu.get_barrier_semaphore(), chips)

    def to_partner(n, source, target):
        return pltpu.make_async_remote_copy(
            src_ref=source, dst_ref=target, send_sem=pair_send.at[n], recv_sem=pair_recv.at[n],
            device_id=partner, device_id_type=pl.DeviceIdType.MESH)

    def to_peer(off, source, target, send, recv):
        place, coords = peer(off)
        return pltpu.make_async_remote_copy(
            src_ref=source.at[place], dst_ref=target.at[here], send_sem=send.at[off],
            recv_sem=recv.at[off], device_id=coords, device_id_type=pl.DeviceIdType.MESH)

    def there(off):
        return to_peer(off, chip, arrived, send_a, recv_a)

    def back(off):
        return to_peer(off, answers, returned, send_b, recv_b)

    def combine(p):
        own, his = send_ref[core * chips + p], other[p]
        before, after = jnp.where(early, own, his), jnp.where(early, his, own)
        pass_on = after[rows:rows + 1]
        return before[:rows] * pass_on + after[:rows], before[rows:] * after[rows:]

    first = to_partner(0, send_ref.at[pl.ds((1 - core) * chips, chips)], other)
    first.start()
    first.wait()

    def put(off):
        place, _ = peer(off)
        total, product = combine(place)
        chip[place, :rows] = total
        chip[place, rows:] = product
        there(off).start()

    each(1, chips, put)
    total, product = combine(here)
    arrived[here, :rows] = total
    arrived[here, rows:] = product
    each(1, chips, lambda off: there(off).wait())

    def step(i, held):
        answers[i] = held
        part = arrived[i]
        return held * part[rows:rows + 1] + part[:rows]

    lax.fori_loop(0, chips, step, jnp.zeros(answers.shape[1:], F32))
    each(1, chips, lambda off: back(off).start())
    returned[here] = answers[here]
    each(1, chips, lambda off: back(off).wait())

    def split(p):
        part = jnp.where(early, send_ref[core * chips + p], other[p])
        enters = returned[p]
        leaves = enters * part[rows:rows + 1] + part[:rows]
        theirs[p] = jnp.where(early, leaves, enters)
        returned[p] = jnp.where(early, enters, leaves)

    each(0, chips, split)
    final = to_partner(1, theirs, last)
    final.start()
    final.wait()
    for half in range(2):
        for p in range(chips):
            pair, g = divmod(half * chips + p, groups)
            out_ref[g * rows:(g + 1) * rows, pair * LANES:(pair + 1) * LANES] = jnp.where(
                core == half, returned[p], last[p])


def output_kernel(count, lengths, x_ref, decay_ref, b_ref, c_ref, incoming_ref, enter_ref,
                  before_ref, gain_ref, score_ref, steps_ref, y_ref, part_ref,
                  spread, gain, starts):
    k = pl.program_id(0)
    heads, width = decay_ref.shape[0], x_ref.shape[1]
    lines = steps_ref.shape[0]

    @pl.when(k == 0)
    def _():
        spread[...] = spread_matrix(heads, width)
        gain[...] = jnp.dot(halves(jnp.broadcast_to(gain_ref[...], (16, heads))), spread[...],
                            preferred_element_type=F32)[:8]
        sizes = steps_ref[...].astype(F32)
        upper = jnp.where(iota((LANES, LANES), 0) < iota((LANES, LANES), 1), 1.0, 0.0).astype(F32)
        inner = jnp.dot(sizes, upper, precision=lax.Precision.HIGHEST, preferred_element_type=F32)
        total = jnp.sum(sizes, axis=1, keepdims=True)
        offset = jnp.zeros((1, 1), F32)
        for i in range(lines):
            starts[i:i + 1, :] = inner[i:i + 1, :] + offset
            offset = offset + total[i:i + 1, :]
        part_ref[...] = jnp.zeros_like(part_ref)

    for sub in range(OUTPUT_CHUNKS):
        first = (my_index() * count + k * OUTPUT_CHUNKS + sub) * CHUNK
        tokens = slice(sub * CHUNK, (sub + 1) * CHUNK)
        cum_rows = running(decay_ref[:, tokens])
        cum = cum_rows.T
        c = c_ref[:, tokens].T
        trace = trace_at(lengths, first + iota((CHUNK, 1), 0))
        trace_row = trace_at(lengths, first + iota((1, CHUNK), 1))
        prev_trace = trace_at(lengths, jnp.full((1, 1), first - 1, jnp.int32))
        keep = (iota((CHUNK, CHUNK), 0) >= iota((CHUNK, CHUNK), 1)) & (trace == trace_row)
        gram = jnp.dot(c, b_ref[:, tokens], preferred_element_type=F32)
        gram = jnp.where(keep, gram, 0.0)
        c_kept = jnp.where(trace == prev_trace, c.astype(F32), 0.0).astype(BF16)
        low_half = iota((CHUNK, LANES), 1) < LANES // 2
        quad = 2 * LANES
        scores = jnp.zeros((CHUNK, LANES), F32)

        def weight(h):
            here = jnp.broadcast_to(cum[:, h:h + 1], (CHUNK, CHUNK))
            diff = jnp.minimum(here - cum_rows[h:h + 1, :], 0.0)
            return here, (gram * jnp.exp2(diff)).astype(BF16)

        for q in range(width // quad):
            wide = slice(q * quad, (q + 1) * quad)
            full = (before_ref[sub, :1, wide] * incoming_ref[:, wide]
                    + enter_ref[sub, :, wide].astype(F32)).astype(BF16)
            inter = jnp.dot(c_kept, full, preferred_element_type=F32)
            for half in range(2):
                pair = 2 * q + half
                columns = slice(pair * LANES, (pair + 1) * LANES)
                x_pair = x_ref[tokens, columns]
                zero = jnp.zeros_like(x_pair)
                both = jnp.concatenate(
                    [jnp.where(low_half, x_pair, zero), jnp.where(low_half, zero, x_pair)], axis=0)
                here_a, weight_a = weight(2 * pair)
                here_b, weight_b = weight(2 * pair + 1)
                intra = jnp.dot(jnp.concatenate([weight_a, weight_b], axis=1), both,
                                preferred_element_type=F32)
                carry = jnp.exp2(jnp.where(low_half, here_a, here_b))
                y = (intra + carry * inter[:, half * LANES:(half + 1) * LANES]
                     + gain[:1, columns] * x_pair.astype(F32)).astype(BF16)
                y_ref[tokens, columns] = y
                scores = scores + y.astype(F32) * score_ref[:1, columns].astype(F32)

        score = jnp.sum(scores, axis=1, keepdims=True)
        places = (first + iota((CHUNK, 1), 0)).astype(F32)
        sizes = steps_ref[...].astype(F32)
        for i in range(lines):
            start = starts[i:i + 1, :]
            inside = (start <= places) & (places < start + sizes[i:i + 1, :])
            part_ref[i:i + 1, :] += jnp.sum(jnp.where(inside, score, 0.0), axis=0, keepdims=True)


def pool_kernel(owned, part_ref, steps_ref, slot_ref, out_ref, near, sums, far,
                send_a, recv_a, send_b, recv_b):
    sec, dev = lax.axis_index("sec"), lax.axis_index("dev")
    secs, devs = lax.axis_size("sec"), lax.axis_size("dev")
    lines = steps_ref.shape[0]

    def beside(off):
        return (sec, wrapped(dev + off, devs))

    def across(off):
        return (wrapped(sec + off, secs), dev)

    def inner(off):
        return pltpu.make_async_remote_copy(
            src_ref=part_ref, dst_ref=near.at[dev], send_sem=send_a.at[off],
            recv_sem=recv_a.at[off], device_id=beside(off), device_id_type=pl.DeviceIdType.MESH)

    def outer(off):
        return pltpu.make_async_remote_copy(
            src_ref=sums, dst_ref=far.at[sec], send_sem=send_b.at[off],
            recv_sem=recv_b.at[off], device_id=across(off), device_id_type=pl.DeviceIdType.MESH)

    each(1, devs, lambda off: greet(beside(off)))
    each(1, secs, lambda off: greet(across(off)))
    pl.semaphore_wait(pltpu.get_barrier_semaphore(), devs + secs - 2)
    each(1, devs, lambda off: inner(off).start())
    near[dev] = part_ref[...]
    each(1, devs, lambda off: inner(off).wait())
    sums[...] = jnp.sum(near[...], axis=0)
    each(1, secs, lambda off: outer(off).start())
    far[sec] = sums[...]
    each(1, secs, lambda off: outer(off).wait())
    mean = jnp.sum(far[...], axis=0)[:lines] / steps_ref[...].astype(F32)
    slots = my_index() * owned + iota((owned, LANES), 0)
    found = jnp.zeros((owned, LANES), F32)
    for i in range(lines):
        found = found + jnp.where(slot_ref[i:i + 1, :] == slots, mean[i:i + 1, :], 0.0)
    out_ref[...] = jnp.broadcast_to(jnp.sum(found, axis=1, keepdims=True), (owned, LANES))


def shards(x_input, log_decay, b_input, c_input, skip_gain, score_weight, trace_lengths,
           step_lengths, step_slot):
    rows, width = x_input.shape
    heads = log_decay.shape[1]
    state_size = b_input.shape[1]
    count = rows // CHUNK
    devices = lax.axis_size(("sec", "dev"))
    groups = devices // (width // LANES)
    depth = state_size // groups
    steps = step_slot.shape[0]
    lines = steps // LANES
    owned = steps // devices
    whole = pl.BlockSpec(memory_space=pltpu.VMEM)
    scalar = pl.BlockSpec(memory_space=pltpu.SMEM)

    chips = devices // 2
    sections, across = lax.axis_size("sec"), lax.axis_size("dev")
    decay_rows, b_rows, c_rows = log_decay.T, b_input.T, c_input.T

    def by_chunk(n):
        return pl.BlockSpec((n * CHUNK, width), lambda k: (k, 0))

    def by_row(n, lines):
        return pl.BlockSpec((lines, n * CHUNK), lambda k: (0, k))

    def by_chunk3(n, a, b):
        return pl.BlockSpec((n, a, b), lambda k: (k, 0, 0))

    def fixed(*shape):
        return pl.BlockSpec(shape, lambda k: (0,) * len(shape))

    enter, before, send = pl.pallas_call(
        functools.partial(state_kernel, count, groups),
        grid=(count // STATE_CHUNKS,),
        in_specs=[scalar, by_chunk(STATE_CHUNKS), by_row(STATE_CHUNKS, heads),
                  by_row(STATE_CHUNKS, state_size)],
        out_specs=[by_chunk3(STATE_CHUNKS, state_size, width), by_chunk3(STATE_CHUNKS, 8, width),
                   fixed(devices, depth + 8, LANES)],
        out_shape=[jax.ShapeDtypeStruct((count, state_size, width), BF16),
                   jax.ShapeDtypeStruct((count, 8, width), F32),
                   jax.ShapeDtypeStruct((devices, depth + 8, LANES), F32)],
        scratch_shapes=[pltpu.VMEM((2 * heads, width), BF16), pltpu.VMEM((state_size, width), F32),
                        pltpu.VMEM((8, width), F32)],
        compiler_params=pltpu.CompilerParams(vmem_limit_bytes=VMEM_BYTES),
        name="chunk_states",
    )(trace_lengths, x_input, decay_rows, b_rows)

    def sems(n):
        return pltpu.SemaphoreType.DMA((n,))

    def blocks(lines):
        return pltpu.VMEM((chips, lines, LANES), F32)

    incoming = pl.pallas_call(
        functools.partial(exchange_kernel, chips, groups),
        in_specs=[whole],
        out_specs=whole,
        out_shape=jax.ShapeDtypeStruct((state_size, width), F32),
        scratch_shapes=[blocks(depth + 8), blocks(depth + 8), blocks(depth + 8), blocks(depth),
                        blocks(depth), blocks(depth), blocks(depth), sems(2), sems(2),
                        sems(chips), sems(chips), sems(chips), sems(chips)],
        compiler_params=pltpu.CompilerParams(collective_id=0, has_side_effects=True,
                                             vmem_limit_bytes=VMEM_BYTES),
        name="state_exchange",
    )(send)

    lines8 = max(8, lines)
    steps_rows = step_lengths.reshape(lines, LANES)
    y_output, part = pl.pallas_call(
        functools.partial(output_kernel, count),
        grid=(count // OUTPUT_CHUNKS,),
        in_specs=[scalar, by_chunk(OUTPUT_CHUNKS), by_row(OUTPUT_CHUNKS, heads),
                  by_row(OUTPUT_CHUNKS, state_size), by_row(OUTPUT_CHUNKS, state_size),
                  fixed(state_size, width), by_chunk3(OUTPUT_CHUNKS, state_size, width),
                  by_chunk3(OUTPUT_CHUNKS, 8, width), fixed(1, heads), fixed(1, width), fixed(lines, LANES)],
        out_specs=[by_chunk(OUTPUT_CHUNKS), fixed(lines8, LANES)],
        out_shape=[jax.ShapeDtypeStruct((rows, width), BF16),
                   jax.ShapeDtypeStruct((lines8, LANES), F32)],
        scratch_shapes=[pltpu.VMEM((2 * heads, width), BF16), pltpu.VMEM((8, width), F32),
                        pltpu.VMEM((lines8, LANES), F32)],
        compiler_params=pltpu.CompilerParams(vmem_limit_bytes=VMEM_BYTES),
        name="outputs",
    )(trace_lengths, x_input, decay_rows, b_rows, c_rows, incoming, enter, before,
      skip_gain.reshape(1, heads), score_weight.reshape(1, width), steps_rows)

    pooled = pl.pallas_call(
        functools.partial(pool_kernel, owned),
        in_specs=[whole, whole, whole],
        out_specs=whole,
        out_shape=jax.ShapeDtypeStruct((owned, LANES), F32),
        scratch_shapes=[pltpu.VMEM((across, lines8, LANES), F32), pltpu.VMEM((lines8, LANES), F32),
                        pltpu.VMEM((sections, lines8, LANES), F32), sems(across), sems(across),
                        sems(sections), sems(sections)],
        compiler_params=pltpu.CompilerParams(collective_id=1, has_side_effects=True,
                                             vmem_limit_bytes=VMEM_BYTES),
        name="step_pool",
    )(part, steps_rows, step_slot.reshape(lines, LANES))
    return (y_output, pooled[:, 0])


def solution(mesh):
    tokens = P(("sec", "dev"), None)
    return jax.shard_map(
        shards,
        mesh=mesh,
        in_specs=(tokens, tokens, tokens, tokens, P(), P(), P(), P(), P()),
        out_specs=(tokens, P(("sec", "dev"))),
        check_vma=False,
    )
```

```python
import functools
import math

import jax
import jax.numpy as jnp
from jax import lax
from jax.experimental import pallas as pl
from jax.experimental.pallas import tpu as pltpu
from jax.sharding import PartitionSpec as P

CHUNK = 128
STATE_CHUNKS = 4
OUTPUT_CHUNKS = 2
LANES = 128
LOG2E = 1.0 / math.log(2.0)
F32 = jnp.float32
BF16 = jnp.bfloat16
VMEM_BYTES = 60 * 1024 * 1024


def iota(shape, dim):
    return lax.broadcasted_iota(jnp.int32, shape, dim)


def my_index():
    return lax.axis_index("sec") * lax.axis_size("dev") + lax.axis_index("dev")


def trace_at(lengths_ref, positions):
    start = jnp.int32(0)
    found = jnp.zeros(jnp.shape(positions), jnp.int32)
    for i in range(lengths_ref.shape[0]):
        found = found + jnp.where(positions >= start, 1, 0)
        start = start + lengths_ref[i]
    return found


def running(decay_rows):
    ones = jnp.where(iota((CHUNK, CHUNK), 0) <= iota((CHUNK, CHUNK), 1), 1.0, 0.0).astype(F32)
    cum = jnp.dot(decay_rows, ones, precision=lax.Precision.HIGHEST, preferred_element_type=F32)
    return cum * LOG2E


def halves(value):
    high = value.astype(BF16)
    low = (value - high.astype(F32)).astype(BF16)
    return jnp.concatenate([high, low], axis=1)


def spread_matrix(heads, width):
    size = width // heads
    row = iota((2 * heads, width), 0)
    head = jnp.where(row >= heads, row - heads, row)
    column = iota((2 * heads, width), 1)
    inside = (column >= head * size) & (column < (head + 1) * size)
    return jnp.where(inside, 1.0, 0.0).astype(BF16)


def state_kernel(count, groups, lengths, x_ref, decay_ref, b_ref, c_ref, gain_ref, enter_ref,
                 before_ref, send_ref, gram_ref, cum_ref, rows_ref, wide_gain_ref,
                 spread, state, factor):
    k = pl.program_id(0)
    heads, width = decay_ref.shape[0], x_ref.shape[1]

    @pl.when(k == 0)
    def _():
        spread[...] = spread_matrix(heads, width)
        state[...] = jnp.zeros_like(state)
        factor[...] = jnp.ones_like(factor)
        wide_gain_ref[...] = jnp.dot(halves(jnp.broadcast_to(gain_ref[...], (16, heads))),
                                     spread[...], preferred_element_type=F32)[:8]

    ends, passes = [], jnp.zeros((heads, LANES), F32)
    for sub in range(STATE_CHUNKS):
        tokens = slice(sub * CHUNK, (sub + 1) * CHUNK)
        first = (my_index() * count + k * STATE_CHUNKS + sub) * CHUNK
        cum = running(decay_ref[:, tokens])
        trace = trace_at(lengths, first + iota((1, CHUNK), 1))
        last_trace = trace_at(lengths, jnp.full((1, 1), first + CHUNK - 1, jnp.int32))
        prev_trace = trace_at(lengths, jnp.full((1, 1), first - 1, jnp.int32))
        rows_ref[:, tokens] = cum
        cum_ref[tokens, :] = cum.T
        trace_column = trace_at(lengths, first + iota((CHUNK, 1), 0))
        keep = (iota((CHUNK, CHUNK), 0) >= iota((CHUNK, CHUNK), 1)) & (trace_column == trace)
        gram = jnp.dot(c_ref[:, tokens].T, b_ref[:, tokens], preferred_element_type=F32)
        gram_ref[tokens, :] = jnp.where(keep, gram, 0.0)
        end = cum[:, CHUNK - 1:]
        ends.append(jnp.exp2(end - cum) * jnp.where(trace == last_trace, 1.0, 0.0))
        through = jnp.exp2(end) * jnp.where(last_trace == prev_trace, 1.0, 0.0)
        passes = passes + jnp.where(iota((heads, LANES), 1) == sub, through, 0.0)
    pass_on = jnp.dot(halves(passes.T[:16]), spread[...], preferred_element_type=F32)

    inputs = [b_ref[:, sub * CHUNK:(sub + 1) * CHUNK].astype(F32) for sub in range(STATE_CHUNKS)]
    states = state.shape[0]
    low_half = iota((states, LANES), 1) < LANES // 2
    for pair in range(width // LANES):
        columns = slice(pair * LANES, (pair + 1) * LANES)
        held, product = state[:, columns], factor[:, columns]
        for sub in range(STATE_CHUNKS):
            tokens = slice(sub * CHUNK, (sub + 1) * CHUNK)
            both = jnp.concatenate(
                [(inputs[sub] * ends[sub][h:h + 1, :]).astype(BF16) for h in (2 * pair, 2 * pair + 1)],
                axis=0)
            new = jnp.dot(both, x_ref[tokens, columns], preferred_element_type=F32)
            step = pass_on[sub:sub + 1, columns]
            enter_ref[sub, :, columns] = held.astype(BF16)
            before_ref[sub, :, columns] = product
            held = held * step + jnp.where(low_half, new[:states], new[states:])
            product = product * step
        state[:, columns] = held
        factor[:, columns] = product

    @pl.when(k == count // STATE_CHUNKS - 1)
    def _():
        rows = state.shape[0] // groups
        for pair in range(width // LANES):
            columns = slice(pair * LANES, (pair + 1) * LANES)
            for g in range(groups):
                send_ref[pair * groups + g, :rows, :] = state[g * rows:(g + 1) * rows, columns]
                send_ref[pair * groups + g, rows:, :] = factor[:, columns]


def wrapped(index, size):
    return index - jnp.where(index >= size, size, 0)


def each(low, high, action):
    def one(i, _):
        action(i)
        return 0

    lax.fori_loop(low, high, one, 0)


def greet(coords):
    pl.semaphore_signal(pltpu.get_barrier_semaphore(), inc=1, device_id=coords,
                        device_id_type=pl.DeviceIdType.MESH)


def inside_chunk(k, x, gram_ref, cum_ref, rows_ref, gain_ref, held):
    tokens = pl.ds(pl.multiple_of(k * CHUNK, CHUNK), CHUNK)
    gram, cum, cum_rows = gram_ref[tokens, :], cum_ref[tokens, :], rows_ref[:, tokens]
    low_half = iota((CHUNK, LANES), 1) < LANES // 2

    def weight(h):
        diff = jnp.minimum(cum[:, h:h + 1] - cum_rows[h:h + 1, :], 0.0)
        return (gram * jnp.exp2(diff)).astype(BF16)

    for pair in range(x.shape[1] // LANES):
        columns = slice(pair * LANES, (pair + 1) * LANES)
        x_pair = x[tokens, columns]
        zero = jnp.zeros_like(x_pair)
        both = jnp.concatenate(
            [jnp.where(low_half, x_pair, zero), jnp.where(low_half, zero, x_pair)], axis=0)
        weights = jnp.concatenate([weight(2 * pair), weight(2 * pair + 1)], axis=1)
        held[tokens, columns] = (jnp.dot(weights, both, preferred_element_type=F32)
                                 + gain_ref[:1, columns] * x_pair.astype(F32))


def exchange_kernel(chips, groups, send_ref, gram_ref, cum_ref, rows_ref, gain_ref, x_ref,
                    out_ref, inner_ref, x, held, load, store, other, chip, arrived, answers, returned,
                    theirs, last, pair_send, pair_recv, send_a, recv_a, send_b, recv_b):
    sec, dev = lax.axis_index("sec"), lax.axis_index("dev")
    per_sec = lax.axis_size("dev") // 2
    core = lax.rem(dev, 2)
    here = sec * per_sec + lax.div(dev, 2)
    early = core == 0
    count = x.shape[0] // CHUNK
    first_part = (count * 9) // 16
    loading = pltpu.make_async_copy(x_ref, x, load.at[0])
    loading.start()
    partner = (sec, dev + 1 - 2 * core)
    rows = answers.shape[1]

    def peer(off):
        place = wrapped(here + off, chips)
        return place, (lax.div(place, per_sec), lax.rem(place, per_sec) * 2 + core)

    each(1, chips, lambda off: greet(peer(off)[1]))
    greet(partner)
    pl.semaphore_wait(pltpu.get_barrier_semaphore(), chips)

    def save(k):
        tokens = pl.ds(pl.multiple_of(k * CHUNK, CHUNK), CHUNK)
        return pltpu.make_async_copy(held.at[tokens], inner_ref.at[tokens], store.at[k])

    def compute(k):
        inside_chunk(k, x, gram_ref, cum_ref, rows_ref, gain_ref, held)
        save(k).start()

    def to_partner(n, source, target):
        return pltpu.make_async_remote_copy(
            src_ref=source, dst_ref=target, send_sem=pair_send.at[n], recv_sem=pair_recv.at[n],
            device_id=partner, device_id_type=pl.DeviceIdType.MESH)

    def to_peer(off, source, target, send, recv):
        place, coords = peer(off)
        return pltpu.make_async_remote_copy(
            src_ref=source.at[place], dst_ref=target.at[here], send_sem=send.at[off],
            recv_sem=recv.at[off], device_id=coords, device_id_type=pl.DeviceIdType.MESH)

    def there(off):
        return to_peer(off, chip, arrived, send_a, recv_a)

    def back(off):
        return to_peer(off, answers, returned, send_b, recv_b)

    def combine(p):
        own, his = send_ref[core * chips + p], other[p]
        before, after = jnp.where(early, own, his), jnp.where(early, his, own)
        pass_on = after[rows:rows + 1]
        return before[:rows] * pass_on + after[:rows], before[rows:] * after[rows:]

    first = to_partner(0, send_ref.at[pl.ds((1 - core) * chips, chips)], other)
    first.start()
    first.wait()

    def put(off):
        place, _ = peer(off)
        total, product = combine(place)
        chip[place, :rows] = total
        chip[place, rows:] = product
        there(off).start()

    each(1, chips, put)
    total, product = combine(here)
    arrived[here, :rows] = total
    arrived[here, rows:] = product
    loading.wait()
    each(0, first_part, compute)
    each(1, chips, lambda off: there(off).wait())

    def step(i, held):
        answers[i] = held
        part = arrived[i]
        return held * part[rows:rows + 1] + part[:rows]

    lax.fori_loop(0, chips, step, jnp.zeros(answers.shape[1:], F32))
    each(1, chips, lambda off: back(off).start())
    returned[here] = answers[here]
    each(first_part, count, compute)
    each(1, chips, lambda off: back(off).wait())

    def split(p):
        part = jnp.where(early, send_ref[core * chips + p], other[p])
        enters = returned[p]
        leaves = enters * part[rows:rows + 1] + part[:rows]
        theirs[p] = jnp.where(early, leaves, enters)
        returned[p] = jnp.where(early, enters, leaves)

    each(0, chips, split)
    final = to_partner(1, theirs, last)
    final.start()
    final.wait()
    for half in range(2):
        for p in range(chips):
            pair, g = divmod(half * chips + p, groups)
            out_ref[g * rows:(g + 1) * rows, pair * LANES:(pair + 1) * LANES] = jnp.where(
                core == half, returned[p], last[p])
    each(0, count, lambda k: save(k).wait())


def output_kernel(count, lengths, inner_ref, cum_ref, c_ref, incoming_ref, enter_ref,
                  before_ref, score_ref, steps_ref, y_ref, part_ref, spread, starts):
    k = pl.program_id(0)
    heads, width = cum_ref.shape[1], inner_ref.shape[1]
    lines = steps_ref.shape[0]

    @pl.when(k == 0)
    def _():
        spread[...] = spread_matrix(heads, width)
        sizes = steps_ref[...].astype(F32)
        upper = jnp.where(iota((LANES, LANES), 0) < iota((LANES, LANES), 1), 1.0, 0.0).astype(F32)
        inner = jnp.dot(sizes, upper, precision=lax.Precision.HIGHEST, preferred_element_type=F32)
        total = jnp.sum(sizes, axis=1, keepdims=True)
        offset = jnp.zeros((1, 1), F32)
        for i in range(lines):
            starts[i:i + 1, :] = inner[i:i + 1, :] + offset
            offset = offset + total[i:i + 1, :]
        part_ref[...] = jnp.zeros_like(part_ref)

    quad = 2 * LANES
    for sub in range(OUTPUT_CHUNKS):
        first = (my_index() * count + k * OUTPUT_CHUNKS + sub) * CHUNK
        tokens = slice(sub * CHUNK, (sub + 1) * CHUNK)
        c = c_ref[:, tokens].T
        trace = trace_at(lengths, first + iota((CHUNK, 1), 0))
        prev_trace = trace_at(lengths, jnp.full((1, 1), first - 1, jnp.int32))
        carry = halves(jnp.exp2(cum_ref[tokens, :]) * jnp.where(trace == prev_trace, 1.0, 0.0))
        scores = jnp.zeros((CHUNK, quad), F32)
        for q in range(width // quad):
            columns = slice(q * quad, (q + 1) * quad)
            full = (before_ref[sub, :1, columns] * incoming_ref[:, columns]
                    + enter_ref[sub, :, columns].astype(F32)).astype(BF16)
            inter = jnp.dot(c, full, preferred_element_type=F32)
            wide = jnp.dot(carry, spread[:, columns], preferred_element_type=F32)
            y = (inner_ref[tokens, columns] + wide * inter).astype(BF16)
            y_ref[tokens, columns] = y
            scores = scores + y.astype(F32) * score_ref[:1, columns].astype(F32)

        score = jnp.sum(scores, axis=1, keepdims=True)
        places = (first + iota((CHUNK, 1), 0)).astype(F32)
        sizes = steps_ref[...].astype(F32)
        for i in range(lines):
            start = starts[i:i + 1, :]
            inside = (start <= places) & (places < start + sizes[i:i + 1, :])
            part_ref[i:i + 1, :] += jnp.sum(jnp.where(inside, score, 0.0), axis=0, keepdims=True)


def pool_kernel(owned, part_ref, steps_ref, slot_ref, out_ref, near, sums, far,
                send_a, recv_a, send_b, recv_b):
    sec, dev = lax.axis_index("sec"), lax.axis_index("dev")
    secs, devs = lax.axis_size("sec"), lax.axis_size("dev")
    lines = steps_ref.shape[0]

    def beside(off):
        return (sec, wrapped(dev + off, devs))

    def across(off):
        return (wrapped(sec + off, secs), dev)

    def inner(off):
        return pltpu.make_async_remote_copy(
            src_ref=part_ref, dst_ref=near.at[dev], send_sem=send_a.at[off],
            recv_sem=recv_a.at[off], device_id=beside(off), device_id_type=pl.DeviceIdType.MESH)

    def outer(off):
        return pltpu.make_async_remote_copy(
            src_ref=sums, dst_ref=far.at[sec], send_sem=send_b.at[off],
            recv_sem=recv_b.at[off], device_id=across(off), device_id_type=pl.DeviceIdType.MESH)

    each(1, devs, lambda off: greet(beside(off)))
    each(1, secs, lambda off: greet(across(off)))
    pl.semaphore_wait(pltpu.get_barrier_semaphore(), devs + secs - 2)
    each(1, devs, lambda off: inner(off).start())
    near[dev] = part_ref[...]
    each(1, devs, lambda off: inner(off).wait())
    sums[...] = jnp.sum(near[...], axis=0)
    each(1, secs, lambda off: outer(off).start())
    far[sec] = sums[...]
    each(1, secs, lambda off: outer(off).wait())
    mean = jnp.sum(far[...], axis=0)[:lines] / steps_ref[...].astype(F32)
    slots = my_index() * owned + iota((owned, LANES), 0)
    found = jnp.zeros((owned, LANES), F32)
    for i in range(lines):
        found = found + jnp.where(slot_ref[i:i + 1, :] == slots, mean[i:i + 1, :], 0.0)
    out_ref[...] = jnp.broadcast_to(jnp.sum(found, axis=1, keepdims=True), (owned, LANES))


def shards(x_input, log_decay, b_input, c_input, skip_gain, score_weight, trace_lengths,
           step_lengths, step_slot):
    rows, width = x_input.shape
    heads = log_decay.shape[1]
    state_size = b_input.shape[1]
    count = rows // CHUNK
    devices = lax.axis_size(("sec", "dev"))
    groups = devices // (width // LANES)
    depth = state_size // groups
    steps = step_slot.shape[0]
    lines = steps // LANES
    owned = steps // devices
    whole = pl.BlockSpec(memory_space=pltpu.VMEM)
    scalar = pl.BlockSpec(memory_space=pltpu.SMEM)

    chips = devices // 2
    sections, across = lax.axis_size("sec"), lax.axis_size("dev")
    decay_rows, b_rows, c_rows = log_decay.T, b_input.T, c_input.T

    def by_chunk(n, columns=width):
        return pl.BlockSpec((n * CHUNK, columns), lambda k: (k, 0))

    def by_row(n, lines):
        return pl.BlockSpec((lines, n * CHUNK), lambda k: (0, k))

    def by_chunk3(n, a, b):
        return pl.BlockSpec((n, a, b), lambda k: (k, 0, 0))

    def fixed(*shape):
        return pl.BlockSpec(shape, lambda k: (0,) * len(shape))

    enter, before, send, gram, cum, cum_rows, gain = pl.pallas_call(
        functools.partial(state_kernel, count, groups),
        grid=(count // STATE_CHUNKS,),
        in_specs=[scalar, by_chunk(STATE_CHUNKS), by_row(STATE_CHUNKS, heads),
                  by_row(STATE_CHUNKS, state_size), by_row(STATE_CHUNKS, state_size),
                  fixed(1, heads)],
        out_specs=[by_chunk3(STATE_CHUNKS, state_size, width), by_chunk3(STATE_CHUNKS, 8, width),
                   fixed(devices, depth + 8, LANES), by_chunk(STATE_CHUNKS, CHUNK),
                   by_chunk(STATE_CHUNKS, heads), by_row(STATE_CHUNKS, heads), fixed(8, width)],
        out_shape=[jax.ShapeDtypeStruct((count, state_size, width), BF16),
                   jax.ShapeDtypeStruct((count, 8, width), F32),
                   jax.ShapeDtypeStruct((devices, depth + 8, LANES), F32),
                   jax.ShapeDtypeStruct((rows, CHUNK), F32),
                   jax.ShapeDtypeStruct((rows, heads), F32),
                   jax.ShapeDtypeStruct((heads, rows), F32),
                   jax.ShapeDtypeStruct((8, width), F32)],
        scratch_shapes=[pltpu.VMEM((2 * heads, width), BF16), pltpu.VMEM((state_size, width), F32),
                        pltpu.VMEM((8, width), F32)],
        compiler_params=pltpu.CompilerParams(vmem_limit_bytes=VMEM_BYTES),
        name="chunk_states",
    )(trace_lengths, x_input, decay_rows, b_rows, c_rows, skip_gain.reshape(1, heads))

    def sems(n):
        return pltpu.SemaphoreType.DMA((n,))

    def blocks(lines):
        return pltpu.VMEM((chips, lines, LANES), F32)

    incoming, inner = pl.pallas_call(
        functools.partial(exchange_kernel, chips, groups),
        in_specs=[whole, whole, whole, whole, whole, pl.BlockSpec(memory_space=pl.ANY)],
        out_specs=[whole, pl.BlockSpec(memory_space=pl.ANY)],
        out_shape=[jax.ShapeDtypeStruct((state_size, width), F32),
                   jax.ShapeDtypeStruct((rows, width), F32)],
        scratch_shapes=[pltpu.VMEM((rows, width), BF16), pltpu.VMEM((rows, width), F32),
                        sems(1), sems(count), blocks(depth + 8), blocks(depth + 8), blocks(depth + 8), blocks(depth),
                        blocks(depth), blocks(depth), blocks(depth), sems(2), sems(2),
                        sems(chips), sems(chips), sems(chips), sems(chips)],
        compiler_params=pltpu.CompilerParams(collective_id=0, has_side_effects=True,
                                             vmem_limit_bytes=VMEM_BYTES),
        name="state_exchange",
    )(send, gram, cum, cum_rows, gain, x_input)

    lines8 = max(8, lines)
    steps_rows = step_lengths.reshape(lines, LANES)
    y_output, part = pl.pallas_call(
        functools.partial(output_kernel, count),
        grid=(count // OUTPUT_CHUNKS,),
        in_specs=[scalar, by_chunk(OUTPUT_CHUNKS), by_chunk(OUTPUT_CHUNKS, heads),
                  by_row(OUTPUT_CHUNKS, state_size), fixed(state_size, width),
                  by_chunk3(OUTPUT_CHUNKS, state_size, width), by_chunk3(OUTPUT_CHUNKS, 8, width),
                  fixed(1, width), fixed(lines, LANES)],
        out_specs=[by_chunk(OUTPUT_CHUNKS), fixed(lines8, LANES)],
        out_shape=[jax.ShapeDtypeStruct((rows, width), BF16),
                   jax.ShapeDtypeStruct((lines8, LANES), F32)],
        scratch_shapes=[pltpu.VMEM((2 * heads, width), BF16), pltpu.VMEM((lines8, LANES), F32)],
        compiler_params=pltpu.CompilerParams(vmem_limit_bytes=VMEM_BYTES),
        name="outputs",
    )(trace_lengths, inner, cum, c_rows, incoming, enter, before,
      score_weight.reshape(1, width), steps_rows)

    pooled = pl.pallas_call(
        functools.partial(pool_kernel, owned),
        in_specs=[whole, whole, whole],
        out_specs=whole,
        out_shape=jax.ShapeDtypeStruct((owned, LANES), F32),
        scratch_shapes=[pltpu.VMEM((across, lines8, LANES), F32), pltpu.VMEM((lines8, LANES), F32),
                        pltpu.VMEM((sections, lines8, LANES), F32), sems(across), sems(across),
                        sems(sections), sems(sections)],
        compiler_params=pltpu.CompilerParams(collective_id=1, has_side_effects=True,
                                             vmem_limit_bytes=VMEM_BYTES),
        name="step_pool",
    )(part, steps_rows, step_slot.reshape(lines, LANES))
    return (y_output, pooled[:, 0])


def solution(mesh):
    tokens = P(("sec", "dev"), None)
    return jax.shard_map(
        shards,
        mesh=mesh,
        in_specs=(tokens, tokens, tokens, tokens, P(), P(), P(), P(), P()),
        out_specs=(tokens, P(("sec", "dev"))),
        check_vma=False,
    )
```
